32 devices in a mesh: dp: 8 (over y, x, core), tensor: 4 (over z).
Axes of the slice: x: 2, y: 2, z: 4, core: 2. Of those that a mesh axis runs over, the one named last changes fastest.
Arguments:
- inputs: bfloat16 [2048, 1024], P(('dp', 'tensor')), may hold values from -6 to 6
- first_gain: float32 [1024], replicated, may hold values from 0.1 to 1.9
- entry_projection_weight: bfloat16 [3, 1024, 1024], P(None, 'dp', 'tensor'), may hold values from -0.1875 to 0.1875
- conv_weight: float32 [3, 1024], replicated, may hold values from -3 to 3
- out_weight: bfloat16 [1024, 1024], P('tensor', 'dp'), may hold values from -0.1875 to 0.1875
- second_gain: float32 [1024], replicated, may hold values from 0.1 to 1.9
- gate_up_weight: bfloat16 [2, 1024, 4608], P(None, 'dp', 'tensor'), may hold values from -0.1875 to 0.1875
- down_weight: bfloat16 [4608, 1024], P('tensor', 'dp'), may hold values from -0.09375 to 0.09375
- cotangent: bfloat16 [2048, 1024], P(('dp', 'tensor')), may hold values from -6 to 6
- lengths: int32 [4], replicated, may hold values from 1 to 1024, 2048 in all
Outputs:
- output: bfloat16 [2048, 1024], P(('dp', 'tensor'))
- input_grad: float32 [2048, 1024], P(('dp', 'tensor'))
- first_gain_grad: float32 [1024], replicated
- in_weight_grad: float32 [3, 1024, 1024], P(None, 'dp', 'tensor')
- filter_weight_gradient: float32 [3, 1024], replicated
- out_weight_grad: float32 [1024, 1024], P('tensor', 'dp')
- second_gain_grad: float32 [1024], replicated
- gate_up_grad: float32 [2, 1024, 4608], P(None, 'dp', 'tensor')
- down_grad: float32 [4608, 1024], P('tensor', 'dp')
The draws below stay inside these ranges and needn't reach their ends.
Inputs may be any that keep to these rules, and one draw needn't show every extreme that they name: lengths of the 4 sequences packed end to end in token order; they sum to 2048, and the longest is exactly 1024.
All inputs are finite; a program needn't handle non-finite values.
Results may differ from the reference program's by a relative error of at most 0.012.
Values may be sent and summed in bfloat16 or wider, within the bound.
A program may use at most 128 MiB of HBM per device.

```python
import math
import jax
import jax.numpy as jnp
import numpy as np
from jax import lax

D = 1024
FF = 4608
KERNEL = 3
MAXLEN = 1024
TOKENS = 2048
NSEQ = 4


def with_spikes(values, rng, source, target, parts, factor):
    owner, partner = [(jnp.arange(values.shape[axis_at]) // (values.shape[axis_at] // parts)).reshape([-1 if axis == axis_at else 1 for axis in range(values.ndim)]) for axis_at in (source, target)]
    chosen = jax.random.permutation(rng, parts)[partner]
    strong = (owner == chosen) | (owner == (partner + parts // 2) % parts)
    return jnp.where(strong, factor * values, values)


def block_scale(rng, shape, shards, low, largest):
    def one(axis_at, parts):
        heights = jax.random.uniform(jax.random.fold_in(jax.random.fold_in(rng, 6), axis_at), (parts,), jnp.float32, low / len(shards), largest / len(shards))
        return jnp.repeat(jnp.exp(heights), shape[axis_at] // parts).reshape((-1,) + (1,) * (len(shape) - axis_at - 1))

    loudness = one(*shards[0])
    for cut in shards[1:]:
        loudness = loudness * one(*cut)
    return loudness


def length_profile(count, total, reach, slope):
    weights = [(1 << 20) // math.isqrt(rank ** slope) + 1 for rank in range(2, count + 1)]
    rest, counts = total - reach - (count - 1), [1] * (count - 1)
    while rest > 0:
        free = [i for i in range(count - 1) if counts[i] < reach]
        whole, left = sum([weights[i] for i in free]), rest
        for i in free:
            addition = min(reach - counts[i], max(1, left * weights[i] // whole), rest)
            counts[i] = counts[i] + addition
            rest = rest - addition
    return np.array([reach] + counts)


def uneven_parts(stream_key, amount, total, limit, lean):
    if amount == 2:
        one = jax.random.randint(stream_key, (), max(1, total - limit), min(limit, total - 1) + 1)
        return jnp.stack([one, total - one])
    tallies = jnp.asarray(length_profile(amount, total, limit, lean), jnp.int32)
    couples = (amount - 1) // 2
    source_of, sink = tallies[1:1 + 2 * couples:2], tallies[2:2 + 2 * couples:2]
    room = jnp.minimum(source_of - 1, limit - sink)
    passed = jax.random.randint(jax.random.fold_in(stream_key, 1), (couples,), 0, 1 << 20) % (room + 1)
    tallies = tallies.at[1:1 + 2 * couples:2].set(source_of - passed).at[2:2 + 2 * couples:2].set(sink + passed)
    return tallies[jax.random.permutation(jax.random.fold_in(stream_key, 2), amount)]


def centred(own_key, extent, width, bound, pieces=(), kind=jnp.bfloat16):
    array = width * jax.random.normal(own_key, extent, jnp.float32)
    if pieces:
        array = array * block_scale(own_key, extent, pieces, -0.22, 0.18)
    return jnp.clip(array, -bound, bound).astype(kind)


def noise_with(key, extent, width, limit, shards, heavy, kind=jnp.bfloat16):
    drawn = width * jax.random.normal(key, extent, jnp.float32)
    if shards:
        drawn = drawn * block_scale(key, extent, shards, -0.22, 0.18)
    return jnp.clip(with_spikes(drawn, jax.random.fold_in(key, 3), *heavy), -limit, limit).astype(kind)


def setup_inputs(seed: int = 0) -> dict:
    streams_of = jax.random.split(jax.random.key(seed), 11)
    return {
        "inputs": noise_with(streams_of[0], (TOKENS, D), 1.0, 6.0, ((0, 32),), (0, 1, 32, 2.75)),
        "first_gain": jnp.clip(1.0 + 0.18 * jax.random.normal(streams_of[1], (D,), jnp.float32), 0.1, 1.9),
        "entry_projection_weight": centred(streams_of[2], (3, D, D), D ** -0.5, 0.1875, ((1, 8), (2, 4))),
        "conv_weight": centred(streams_of[3], (KERNEL, D), 0.6, 3.0, (), jnp.float32),
        "out_weight": centred(streams_of[4], (D, D), D ** -0.5, 0.1875, ((0, 4), (1, 8))),
        "second_gain": jnp.clip(1.0 + 0.18 * jax.random.normal(streams_of[5], (D,), jnp.float32), 0.1, 1.9),
        "gate_up_weight": centred(streams_of[6], (2, D, FF), D ** -0.5, 0.1875, ((1, 8), (2, 4))),
        "down_weight": centred(streams_of[7], (FF, D), FF ** -0.5, 0.09375, ((0, 4), (1, 8))),
        "cotangent": noise_with(streams_of[8], (TOKENS, D), 1.0, 6.0, ((0, 32),), (0, 1, 32, 2.75)),
        "lengths": uneven_parts(streams_of[9], NSEQ, TOKENS, MAXLEN, 2).astype(jnp.int32),
    }


EPS = 1e-05
HIGH = lax.Precision.HIGHEST

@jax.custom_vjp
def low(v):
    return lax.optimization_barrier(v.astype(jnp.bfloat16)).astype(jnp.float32)

@jax.custom_vjp
def low_back(v):
    return v

def low_keep(v):
    return (low(v), None)

def low_pass(kept, grad):
    return (grad,)

def back_keep(v):
    return (v, None)

def back_low(kept, grad):
    return (low(grad),)
low.defvjp(low_keep, low_pass)
low_back.defvjp(back_keep, back_low)

def rms_norm(values, gain):
    return values * lax.rsqrt(lax.optimization_barrier(jnp.mean(values * values, axis=-1, keepdims=True)) + EPS) * gain

def matmul(left, right):
    return jnp.dot(left, right, precision=HIGH, preferred_element_type=jnp.float32)

def keep_masks(lengths):
    ends = jnp.cumsum(lengths).astype(jnp.int32)
    places = jnp.arange(TOKENS, dtype=jnp.int32)
    segment = lax.optimization_barrier(jnp.sum((places[:, None] >= ends[None, :]).astype(jnp.int32), axis=1)).astype(jnp.int32)
    first_keep = jnp.concatenate([jnp.zeros((1,), jnp.float32), (segment[1:] == segment[:-1]).astype(jnp.float32)])
    second_keep = jnp.concatenate([jnp.zeros((2,), jnp.float32), (segment[2:] == segment[:-2]).astype(jnp.float32)])
    return (first_keep[:, None], second_keep[:, None])

def forward(inputs, first_gain, entry_projection_weight, conv_weight, out_weight, second_gain, gate_up_weight, down_weight, first_keep, second_keep):
    normed = low(rms_norm(inputs, first_gain))
    input_gate_value = low_back(matmul(normed, entry_projection_weight[0]))
    c_value = low_back(matmul(normed, entry_projection_weight[1]))
    v_value = low_back(matmul(normed, entry_projection_weight[2]))
    product = low(input_gate_value * v_value)
    padded = jnp.concatenate([jnp.zeros((2, D), jnp.float32), product], axis=0)
    mixed = low_back(conv_weight[2] * product + conv_weight[1] * first_keep * padded[1:-1] + conv_weight[0] * second_keep * padded[:-2])
    gated = low(c_value * mixed)
    middle = inputs + low_back(matmul(gated, out_weight))
    block_rows = math.gcd(TOKENS, 4096)

    def feed(block):
        hidden_in = low(rms_norm(block, second_gain))
        gate_value = low_back(matmul(hidden_in, gate_up_weight[0]))
        up_value = low_back(matmul(hidden_in, gate_up_weight[1]))
        hidden = low(jax.nn.silu(gate_value) * up_value)
        return low_back(matmul(hidden, down_weight))
    branch = lax.map(jax.checkpoint(feed), middle.reshape(TOKENS // block_rows, block_rows, D)).reshape(TOKENS, D)
    return middle + branch

def reference(inputs, first_gain, entry_projection_weight, conv_weight, out_weight, second_gain, gate_up_weight, down_weight, cotangent, lengths):
    first_keep, second_keep = keep_masks(lengths)

    def closed(inputs_f, gain_one, in_f, conv_f, out_f, gain_two, gate_up_f, down_f):
        return forward(inputs_f, gain_one, in_f, conv_f, out_f, gain_two, gate_up_f, down_f, first_keep, second_keep)
    result, pullback = jax.vjp(closed, inputs.astype(jnp.float32), first_gain.astype(jnp.float32), entry_projection_weight.astype(jnp.float32), conv_weight.astype(jnp.float32), out_weight.astype(jnp.float32), second_gain.astype(jnp.float32), gate_up_weight.astype(jnp.float32), down_weight.astype(jnp.float32))
    grads = pullback(cotangent.astype(jnp.float32))
    return (result.astype(jnp.bfloat16), grads[0], grads[1], grads[2], grads[3], grads[4], grads[5], grads[6], grads[7])
```

```python
import jax
import jax.numpy as jnp
from jax import lax
from jax.sharding import PartitionSpec as P

EPS = 1e-05


def passed_along(block, axis, distance):
    devices = range(lax.axis_size(axis))
    route = [(i - distance, i) for i in devices if i - distance in devices]
    return lax.ppermute(block, axis, route)


def rms_norm(values, gain):
    return values * lax.rsqrt(jnp.mean(values * values, axis=-1, keepdims=True) + EPS) * gain


def rms_back(values, gain, grad_out):
    scale = lax.rsqrt(jnp.mean(values * values, axis=-1, keepdims=True) + EPS)
    normal = values * scale
    weighted = gain * grad_out
    grad_in = scale * (weighted - normal * jnp.mean(normal * weighted, axis=-1, keepdims=True))
    return (grad_in, jnp.sum(normal * grad_out, axis=0))


def times_trans(left, right):
    return lax.dot_general(
        left, right, (((1,), (1,)), ((), ())), preferred_element_type=jnp.float32
    )


def trans_times(left, right):
    return lax.dot_general(
        left, right, (((0,), (0,)), ((), ())), preferred_element_type=jnp.float32
    )


def swapped(block, axis, mask):
    devices = range(lax.axis_size(axis))
    return lax.ppermute(block, axis, [(i, i ^ mask) for i in devices])


def xor_order(blocks, index):
    bit = 1
    while bit < len(blocks):
        flag = (index & bit) > 0
        blocks = [jnp.where(flag, blocks[j ^ bit], blocks[j]) for j in range(len(blocks))]
        bit *= 2
    return blocks


def order_of(count):
    return list(range(0, count, 2)) + list(range(1, count, 2))


def to_relative(values):
    count = lax.axis_size("dp")
    blocks = xor_order(jnp.split(values, count, axis=-1), lax.axis_index("dp"))
    return jnp.concatenate([blocks[j] for j in order_of(count)], axis=-1)


def to_absolute(values):
    count = lax.axis_size("dp")
    places = jnp.split(values, count, axis=-1)
    blocks = [None] * count
    for place, j in enumerate(order_of(count)):
        blocks[j] = places[place]
    return jnp.concatenate(xor_order(blocks, lax.axis_index("dp")), axis=-1)


def gather_weight(shard, axis, cut):
    count = lax.axis_size("dp")
    if count == 8:
        over_x = swapped(shard, "dp", 2)
        over_y = swapped(shard, "dp", 4)
        first, _ = jnp.split(over_x, 2, axis=cut)
        _, second = jnp.split(over_y, 2, axis=cut)
        corner = jnp.concatenate(
            [swapped(first, "dp", 4), swapped(second, "dp", 2)], axis=cut
        )
        near = jnp.concatenate([shard, over_x, over_y, corner], axis=axis)
    else:
        near = shard
        bit = 2
        while bit < count:
            near = jnp.concatenate([near, swapped(near, "dp", bit)], axis=axis)
            bit *= 2
    return near, swapped(near, "dp", 1)


def wide(values):
    return values.astype(jnp.float32)


def narrow(values):
    return values.astype(jnp.bfloat16)


def scatter_weight(near, far, axis, cut):
    count = lax.axis_size("dp")
    total = wide(near) + wide(swapped(narrow(far), "dp", 1))
    if count == 8:
        own, for_x, for_y, corner = jnp.split(total, 4, axis=axis)
        first, second = jnp.split(narrow(corner), 2, axis=cut)
        got_first = wide(swapped(first, "dp", 2))
        got_second = wide(swapped(second, "dp", 4))
        y_first, y_second = jnp.split(for_y, 2, axis=cut)
        x_first, x_second = jnp.split(for_x, 2, axis=cut)
        for_y = jnp.concatenate([narrow(y_first + got_first), narrow(y_second)], axis=cut)
        for_x = jnp.concatenate([narrow(x_first), narrow(x_second + got_second)], axis=cut)
        return own + wide(swapped(for_x, "dp", 2)) + wide(swapped(for_y, "dp", 4))
    bit = count // 2
    while bit > 1:
        keep, send = jnp.split(total, 2, axis=axis)
        total = keep + wide(swapped(narrow(send), "dp", bit))
        bit //= 2
    return total


def gather_rows(rows):
    return [rows] + [swapped(rows, "tensor", j) for j in range(1, lax.axis_size("tensor"))]


def scatter_rows(blocks):
    total = blocks[0]
    for j in range(1, len(blocks)):
        total = total + wide(swapped(narrow(blocks[j]), "tensor", j))
    return total


def in_token_order(blocks):
    return jnp.concatenate(xor_order(blocks, lax.axis_index("tensor")), axis=0)


def for_owners(rows):
    blocks = jnp.split(rows, lax.axis_size("tensor"), axis=0)
    return xor_order(blocks, lax.axis_index("tensor"))


def summed_over(values, axis):
    count = lax.axis_size(axis)
    if count <= 8:
        blocks = [values] + [swapped(values, axis, j) for j in range(1, count)]
        blocks = xor_order(blocks, lax.axis_index(axis))
        return sum(blocks[1:], blocks[0])
    return lax.psum(values, axis)


def dot(left, right):
    return jnp.dot(left, right, preferred_element_type=jnp.float32)


def halves(values):
    return jnp.split(values, 2, axis=-1)


def shards(
    inputs,
    first_gain,
    entry_projection_weight,
    conv_weight,
    out_weight,
    second_gain,
    gate_up_weight,
    down_weight,
    cotangent,
    lengths,
):
    own_rows = inputs.shape[0]
    group_rows = own_rows * lax.axis_size("tensor")
    channels = entry_projection_weight.shape[2]
    column = lax.axis_index("tensor") * channels
    start = lax.axis_index("dp") * group_rows
    ends = jnp.sum(
        jnp.where(
            jnp.arange(lengths.shape[0])[:, None] >= jnp.arange(lengths.shape[0])[None, :],
            lengths[None, :],
            0,
        ),
        axis=1,
    )
    places = start - 2 + jnp.arange(group_rows + 4, dtype=jnp.int32)
    segment = jnp.sum((places[:, None] >= ends[None, :]).astype(jnp.int32), axis=1)
    first_all = jnp.logical_and(segment[2:] == segment[1:-1], places[2:] >= 1).astype(jnp.float32)[
        :, None
    ]
    second_all = jnp.logical_and(segment[2:] == segment[:-2], places[2:] >= 2).astype(jnp.float32)[
        :, None
    ]
    first_keep = first_all[:group_rows]
    second_keep = second_all[:group_rows]
    kernel = lax.dynamic_slice_in_dim(conv_weight, column, channels, 1)
    residual = wide(to_relative(inputs))
    first_gain = to_relative(first_gain)
    second_gain = to_relative(second_gain)
    cotangent = to_relative(cotangent)

    normed = in_token_order(gather_rows(narrow(rms_norm(residual, first_gain))))
    in_near, in_far = gather_weight(entry_projection_weight, 1, 2)
    out_near, out_far = gather_weight(out_weight, 1, 0)
    gate_up_near, gate_up_far = gather_weight(gate_up_weight, 1, 0)
    down_near, down_far = gather_weight(down_weight, 1, 0)
    grad_rows = jnp.concatenate(gather_rows(cotangent), axis=0)

    normed_near, normed_far = halves(normed)
    projected = [dot(normed_near, in_near[k]) + dot(normed_far, in_far[k]) for k in range(3)]
    input_gate_value, c_value, v_value = projected
    product = narrow(input_gate_value * v_value)
    before = passed_along(product[-2:], "dp", 1)
    extended = wide(jnp.concatenate([before, product], axis=0))
    mixed = (
        kernel[2] * extended[2:]
        + kernel[1] * first_keep * extended[1:-1]
        + kernel[0] * second_keep * extended[:-2]
    )
    gated = narrow(c_value * mixed)
    mixer_part = jnp.concatenate([dot(gated, out_near), dot(gated, out_far)], axis=1)
    middle = residual + scatter_rows(for_owners(mixer_part))
    hidden_in = jnp.concatenate(
        gather_rows(narrow(rms_norm(middle, second_gain))), axis=0
    )
    hidden_near, hidden_far = halves(hidden_in)
    gate_value = dot(hidden_near, gate_up_near[0]) + dot(hidden_far, gate_up_far[0])
    up_value = dot(hidden_near, gate_up_near[1]) + dot(hidden_far, gate_up_far[1])
    sigmoid = jax.nn.sigmoid(gate_value)
    swish = gate_value * sigmoid
    hidden = narrow(swish * up_value)
    grad_near, grad_far = halves(grad_rows)
    down_part_far = narrow(trans_times(hidden, grad_far))
    down_part_near = narrow(trans_times(hidden, grad_near))
    grad_hidden = times_trans(grad_near, down_near) + times_trans(grad_far, down_far)
    grad_gate = narrow(grad_hidden * up_value * sigmoid * (1.0 + gate_value * (1.0 - sigmoid)))
    grad_up = narrow(grad_hidden * swish)
    hidden_back = jnp.concatenate(
        [
            times_trans(grad_gate, half[0]) + times_trans(grad_up, half[1])
            for half in (gate_up_near, gate_up_far)
        ],
        axis=1,
    )
    grad_hin = scatter_rows(jnp.split(hidden_back, lax.axis_size("tensor"), axis=0))
    gate_up_part_far = jnp.stack(
        [narrow(trans_times(hidden_far, grad)) for grad in (grad_gate, grad_up)]
    )
    gate_up_part_near = jnp.stack(
        [narrow(trans_times(hidden_near, grad)) for grad in (grad_gate, grad_up)]
    )
    ffn_part = jnp.concatenate([dot(hidden, down_near), dot(hidden, down_far)], axis=1)
    output = narrow(
        middle + scatter_rows(jnp.split(ffn_part, lax.axis_size("tensor"), axis=0))
    )
    second_back, second_part = rms_back(middle, second_gain, grad_hin)
    grad_middle = wide(cotangent) + second_back
    branch_rows = in_token_order(gather_rows(narrow(grad_middle)))
    branch_near, branch_far = halves(branch_rows)
    grad_gated = times_trans(branch_near, out_near) + times_trans(branch_far, out_far)
    out_part_far = narrow(trans_times(gated, branch_far))
    out_part_near = narrow(trans_times(gated, branch_near))
    output_gate_gradient = narrow(grad_gated * mixed)
    grad_mixed = narrow(grad_gated * c_value)
    after = passed_along(grad_mixed[:2], "dp", -1)
    grad_ext = wide(jnp.concatenate([grad_mixed, after], axis=0))
    mixed_wide = grad_ext[:-2]
    kernel_part = jnp.stack(
        [
            jnp.sum(second_keep * extended[:-2] * mixed_wide, axis=0),
            jnp.sum(first_keep * extended[1:-1] * mixed_wide, axis=0),
            jnp.sum(extended[2:] * mixed_wide, axis=0),
        ]
    )
    kernel_full = lax.dynamic_update_slice_in_dim(
        jnp.zeros(conv_weight.shape, jnp.float32), kernel_part, column, 1
    )
    elementwise_product_gradient = (
        kernel[2] * grad_ext[:-2]
        + kernel[1] * first_all[1:-1] * grad_ext[1:-1]
        + kernel[0] * second_all[2:] * grad_ext[2:]
    )
    input_gate_gradient = narrow(elementwise_product_gradient * v_value)
    value_branch_gradient = narrow(elementwise_product_gradient * input_gate_value)
    grads = [input_gate_gradient, output_gate_gradient, value_branch_gradient]
    in_part_far = jnp.stack([narrow(trans_times(normed_far, grad)) for grad in grads])
    in_part_near = jnp.stack([narrow(trans_times(normed_near, grad)) for grad in grads])
    normed_back = jnp.concatenate(
        [
            sum(times_trans(grads[k], half[k]) for k in range(3))
            for half in (in_near, in_far)
        ],
        axis=1,
    )
    grad_normed = scatter_rows(for_owners(normed_back))
    first_back, first_part = rms_back(residual, first_gain, grad_normed)
    input_grad = grad_middle + first_back
    down_grad = scatter_weight(down_part_near, down_part_far, 1, 0)
    gate_up_grad = scatter_weight(gate_up_part_near, gate_up_part_far, 1, 0)
    out_grad = scatter_weight(out_part_near, out_part_far, 1, 0)
    in_grad = scatter_weight(in_part_near, in_part_far, 1, 2)
    small = jnp.concatenate(
        [to_absolute(first_part)[None], to_absolute(second_part)[None], kernel_full], axis=0
    )
    small = summed_over(summed_over(small, "tensor"), "dp")
    return (
        to_absolute(output),
        to_absolute(input_grad),
        small[0],
        in_grad,
        small[2:],
        out_grad,
        small[1],
        gate_up_grad,
        down_grad,
    )


def solution(mesh):
    in_specs = (
        P(("dp", "tensor"), None),
        P(),
        P(None, "dp", "tensor"),
        P(),
        P("tensor", "dp"),
        P(),
        P(None, "dp", "tensor"),
        P("tensor", "dp"),
        P(("dp", "tensor"), None),
        P(),
    )
    out_specs = (
        P(("dp", "tensor"), None),
        P(("dp", "tensor"), None),
        P(),
        P(None, "dp", "tensor"),
        P(),
        P("tensor", "dp"),
        P(),
        P(None, "dp", "tensor"),
        P("tensor", "dp"),
    )
    return jax.shard_map(shards, mesh=mesh, in_specs=in_specs, out_specs=out_specs, check_vma=False)
```

```python
import jax
import jax.numpy as jnp
from jax import lax
from jax.sharding import PartitionSpec as P

EPS = 1e-05


def passed_along(block, axis, distance):
    devices = range(lax.axis_size(axis))
    route = [(i - distance, i) for i in devices if i - distance in devices]
    return lax.ppermute(block, axis, route)


def rms_norm(values, gain):
    return values * lax.rsqrt(jnp.mean(values * values, axis=-1, keepdims=True) + EPS) * gain


def rms_back(values, gain, grad_out):
    scale = lax.rsqrt(jnp.mean(values * values, axis=-1, keepdims=True) + EPS)
    normal = values * scale
    weighted = gain * grad_out
    grad_in = scale * (weighted - normal * jnp.mean(normal * weighted, axis=-1, keepdims=True))
    return (grad_in, jnp.sum(normal * grad_out, axis=0))


def times_trans(left, right):
    return lax.dot_general(
        left, right, (((1,), (1,)), ((), ())), preferred_element_type=jnp.float32
    )


def trans_times(left, right):
    return lax.dot_general(
        left, right, (((0,), (0,)), ((), ())), preferred_element_type=jnp.float32
    )


def swapped(block, axis, mask):
    devices = range(lax.axis_size(axis))
    return lax.ppermute(block, axis, [(i, i ^ mask) for i in devices])


def xor_order(blocks, index):
    bit = 1
    while bit < len(blocks):
        flag = (index & bit) > 0
        blocks = [jnp.where(flag, blocks[j ^ bit], blocks[j]) for j in range(len(blocks))]
        bit *= 2
    return blocks


def order_of(count):
    return list(range(0, count, 2)) + list(range(1, count, 2))


def to_relative(values):
    count = lax.axis_size("dp")
    blocks = xor_order(jnp.split(values, count, axis=-1), lax.axis_index("dp"))
    return jnp.concatenate([blocks[j] for j in order_of(count)], axis=-1)


def to_absolute(values):
    count = lax.axis_size("dp")
    places = jnp.split(values, count, axis=-1)
    blocks = [None] * count
    for place, j in enumerate(order_of(count)):
        blocks[j] = places[place]
    return jnp.concatenate(xor_order(blocks, lax.axis_index("dp")), axis=-1)


def gather_weight(shard):
    count = lax.axis_size("dp")
    if count == 8:
        over_x, over_y = yield swapped(shard, "dp", 2), swapped(shard, "dp", 4)
        first, _ = jnp.split(over_x, 2, axis=1)
        _, second = jnp.split(over_y, 2, axis=1)
        first, second = yield swapped(first, "dp", 4), swapped(second, "dp", 2)
        near = jnp.concatenate([shard, over_x, over_y, first, second], axis=1)
    else:
        near = shard
        bit = 2
        while bit < count:
            got = yield swapped(near, "dp", bit)
            near = jnp.concatenate([near, got], axis=1)
            bit *= 2
    far = yield swapped(near, "dp", 1)
    yield None, (near, far)


def beside(values, *pending):
    waited = [(steps, held) for steps, held in pending if not finished(held)]
    values, got = lax.optimization_barrier((values, [held for _, held in waited]))
    got = iter(got)
    moved = [
        (steps, held) if finished(held) else (steps, steps.send(next(got)))
        for steps, held in pending
    ]
    return (values, *moved)


def finished(held):
    return isinstance(held, tuple) and held[0] is None


def begin(steps):
    return steps, next(steps)


def finish(steps, held):
    while not finished(held):
        held = steps.send(held)
    return held[1]


def wide(values):
    return values.astype(jnp.float32)


def narrow(values):
    return values.astype(jnp.bfloat16)


def scatter_weight(near, far):
    count = lax.axis_size("dp")
    got = yield swapped(far, "dp", 1)
    total = wide(near) + wide(got)
    if count == 8:
        own, for_x, for_y, corner = jnp.split(total, 4, axis=1)
        first, second = jnp.split(narrow(corner), 2, axis=1)
        first, second = yield swapped(first, "dp", 2), swapped(second, "dp", 4)
        y_first, y_second = jnp.split(for_y, 2, axis=1)
        x_first, x_second = jnp.split(for_x, 2, axis=1)
        for_y = jnp.concatenate([narrow(y_first + wide(first)), narrow(y_second)], axis=1)
        for_x = jnp.concatenate([narrow(x_first), narrow(x_second + wide(second))], axis=1)
        from_x, from_y = yield swapped(for_x, "dp", 2), swapped(for_y, "dp", 4)
        total = own + wide(from_x) + wide(from_y)
    else:
        bit = count // 2
        while bit > 1:
            keep, send = jnp.split(total, 2, axis=1)
            got = yield swapped(narrow(send), "dp", bit)
            total = keep + wide(got)
            bit //= 2
    yield None, total


def gather_rows(rows):
    return [rows] + [swapped(rows, "tensor", j) for j in range(1, lax.axis_size("tensor"))]


def scatter_rows(blocks):
    total = blocks[0]
    for j in range(1, len(blocks)):
        total = total + wide(swapped(narrow(blocks[j]), "tensor", j))
    return total


def in_token_order(blocks):
    return jnp.concatenate(xor_order(blocks, lax.axis_index("tensor")), axis=0)


def for_owners(rows):
    blocks = jnp.split(rows, lax.axis_size("tensor"), axis=0)
    return xor_order(blocks, lax.axis_index("tensor"))


def summed_over(values, axis):
    count = lax.axis_size(axis)
    if count <= 8:
        blocks = [values] + [swapped(values, axis, j) for j in range(1, count)]
        blocks = xor_order(blocks, lax.axis_index(axis))
        return sum(blocks[1:], blocks[0])
    return lax.psum(values, axis)


def dot(left, right):
    return jnp.dot(left, right, preferred_element_type=jnp.float32)


def halves(values):
    return jnp.split(values, 2, axis=-1)


def shards(
    inputs,
    first_gain,
    entry_projection_weight,
    conv_weight,
    out_weight,
    second_gain,
    gate_up_weight,
    down_weight,
    cotangent,
    lengths,
):
    own_rows = inputs.shape[0]
    group_rows = own_rows * lax.axis_size("tensor")
    channels = entry_projection_weight.shape[2]
    column = lax.axis_index("tensor") * channels
    start = lax.axis_index("dp") * group_rows
    ends = jnp.sum(
        jnp.where(
            jnp.arange(lengths.shape[0])[:, None] >= jnp.arange(lengths.shape[0])[None, :],
            lengths[None, :],
            0,
        ),
        axis=1,
    )
    places = start - 2 + jnp.arange(group_rows + 4, dtype=jnp.int32)
    segment = jnp.sum((places[:, None] >= ends[None, :]).astype(jnp.int32), axis=1)
    first_all = jnp.logical_and(segment[2:] == segment[1:-1], places[2:] >= 1).astype(jnp.float32)[
        :, None
    ]
    second_all = jnp.logical_and(segment[2:] == segment[:-2], places[2:] >= 2).astype(jnp.float32)[
        :, None
    ]
    first_keep = first_all[:group_rows]
    second_keep = second_all[:group_rows]
    kernel = lax.dynamic_slice_in_dim(conv_weight, column, channels, 1)
    residual = wide(to_relative(inputs))
    first_gain = to_relative(first_gain)
    second_gain = to_relative(second_gain)
    cotangent = to_relative(cotangent)

    mixer_weights = jnp.concatenate([entry_projection_weight, out_weight.T[None]], axis=0)
    ffn_weights = jnp.concatenate([gate_up_weight, down_weight.T[None]], axis=0)
    mixer_gather = begin(gather_weight(mixer_weights))
    normed_parts = gather_rows(narrow(rms_norm(residual, first_gain)))
    normed_parts, mixer_gather = beside(normed_parts, mixer_gather)
    ffn_weights, mixer_gather = beside(ffn_weights, mixer_gather)
    ffn_gather = begin(gather_weight(ffn_weights))
    grad_parts = gather_rows(cotangent)
    mixer_near, mixer_far = finish(*mixer_gather)
    normed = in_token_order(normed_parts)

    normed_near, normed_far = halves(normed)
    projected = [
        dot(normed_near, mixer_near[k]) + dot(normed_far, mixer_far[k]) for k in range(3)
    ]
    input_gate_value, c_value, v_value = projected
    product = narrow(input_gate_value * v_value)
    before = passed_along(product[-2:], "dp", 1)
    extended = wide(jnp.concatenate([before, product], axis=0))
    mixed = (
        kernel[2] * extended[2:]
        + kernel[1] * first_keep * extended[1:-1]
        + kernel[0] * second_keep * extended[:-2]
    )
    gated = narrow(c_value * mixed)
    gated, ffn_gather = beside(gated, ffn_gather)
    mixer_part = jnp.concatenate(
        [times_trans(gated, mixer_near[3]), times_trans(gated, mixer_far[3])], axis=1
    )
    middle = residual + scatter_rows(for_owners(mixer_part))
    (middle, grad_parts), ffn_gather = beside((middle, grad_parts), ffn_gather)
    grad_rows = jnp.concatenate(grad_parts, axis=0)
    hidden_in = jnp.concatenate(
        gather_rows(narrow(rms_norm(middle, second_gain))), axis=0
    )
    hidden_near, hidden_far = halves(hidden_in)
    ffn_near, ffn_far = finish(*ffn_gather)
    gate_value = dot(hidden_near, ffn_near[0]) + dot(hidden_far, ffn_far[0])
    up_value = dot(hidden_near, ffn_near[1]) + dot(hidden_far, ffn_far[1])
    sigmoid = jax.nn.sigmoid(gate_value)
    swish = gate_value * sigmoid
    hidden = narrow(swish * up_value)
    grad_near, grad_far = halves(grad_rows)
    grad_hidden = dot(grad_near, ffn_near[2]) + dot(grad_far, ffn_far[2])
    grad_gate = narrow(grad_hidden * up_value * sigmoid * (1.0 + gate_value * (1.0 - sigmoid)))
    grad_up = narrow(grad_hidden * swish)
    hidden_back = jnp.concatenate(
        [
            times_trans(grad_gate, half[0]) + times_trans(grad_up, half[1])
            for half in (ffn_near, ffn_far)
        ],
        axis=1,
    )
    ffn_scatter = begin(
        scatter_weight(
            *[
                jnp.stack(
                    [
                        narrow(trans_times(rows, grad_gate)),
                        narrow(trans_times(rows, grad_up)),
                        narrow(trans_times(outer, hidden)),
                    ]
                )
                for rows, outer in ((hidden_near, grad_near), (hidden_far, grad_far))
            ]
        )
    )
    grad_hin = scatter_rows(jnp.split(hidden_back, lax.axis_size("tensor"), axis=0))
    grad_hin, ffn_scatter = beside(grad_hin, ffn_scatter)
    second_back, second_part = rms_back(middle, second_gain, grad_hin)
    grad_middle = wide(cotangent) + second_back
    branch_rows = in_token_order(gather_rows(narrow(grad_middle)))
    (branch_rows, hidden), ffn_scatter = beside((branch_rows, hidden), ffn_scatter)
    ffn_part = jnp.concatenate(
        [times_trans(hidden, ffn_near[2]), times_trans(hidden, ffn_far[2])], axis=1
    )
    output = narrow(
        middle + scatter_rows(jnp.split(ffn_part, lax.axis_size("tensor"), axis=0))
    )
    branch_near, branch_far = halves(branch_rows)
    grad_gated = dot(branch_near, mixer_near[3]) + dot(branch_far, mixer_far[3])
    output_gate_gradient = narrow(grad_gated * mixed)
    grad_mixed = narrow(grad_gated * c_value)
    after = passed_along(grad_mixed[:2], "dp", -1)
    grad_ext = wide(jnp.concatenate([grad_mixed, after], axis=0))
    mixed_wide = grad_ext[:-2]
    kernel_part = jnp.stack(
        [
            jnp.sum(second_keep * extended[:-2] * mixed_wide, axis=0),
            jnp.sum(first_keep * extended[1:-1] * mixed_wide, axis=0),
            jnp.sum(extended[2:] * mixed_wide, axis=0),
        ]
    )
    kernel_full = lax.dynamic_update_slice_in_dim(
        jnp.zeros(conv_weight.shape, jnp.float32), kernel_part, column, 1
    )
    elementwise_product_gradient = (
        kernel[2] * grad_ext[:-2]
        + kernel[1] * first_all[1:-1] * grad_ext[1:-1]
        + kernel[0] * second_all[2:] * grad_ext[2:]
    )
    input_gate_gradient = narrow(elementwise_product_gradient * v_value)
    value_branch_gradient = narrow(elementwise_product_gradient * input_gate_value)
    grads = [input_gate_gradient, output_gate_gradient, value_branch_gradient]
    mixer_scatter = begin(
        scatter_weight(
            *[
                jnp.stack(
                    [narrow(trans_times(rows, grad)) for grad in grads]
                    + [narrow(trans_times(outer, gated))]
                )
                for rows, outer in ((normed_near, branch_near), (normed_far, branch_far))
            ]
        )
    )
    normed_back = jnp.concatenate(
        [
            sum(times_trans(grads[k], half[k]) for k in range(3))
            for half in (mixer_near, mixer_far)
        ],
        axis=1,
    )
    grad_normed = scatter_rows(for_owners(normed_back))
    (grad_normed, output), ffn_scatter, mixer_scatter = beside(
        (grad_normed, output), ffn_scatter, mixer_scatter
    )
    first_back, first_part = rms_back(residual, first_gain, grad_normed)
    input_grad = grad_middle + first_back
    ffn_grad = finish(*ffn_scatter)
    mixer_grad = finish(*mixer_scatter)
    small = jnp.concatenate(
        [to_absolute(first_part)[None], to_absolute(second_part)[None], kernel_full], axis=0
    )
    small = summed_over(summed_over(small, "tensor"), "dp")
    return (
        to_absolute(output),
        to_absolute(input_grad),
        small[0],
        mixer_grad[:3],
        small[2:],
        mixer_grad[3].T,
        small[1],
        ffn_grad[:2],
        ffn_grad[2].T,
    )


def solution(mesh):
    in_specs = (
        P(("dp", "tensor"), None),
        P(),
        P(None, "dp", "tensor"),
        P(),
        P("tensor", "dp"),
        P(),
        P(None, "dp", "tensor"),
        P("tensor", "dp"),
        P(("dp", "tensor"), None),
        P(),
    )
    out_specs = (
        P(("dp", "tensor"), None),
        P(("dp", "tensor"), None),
        P(),
        P(None, "dp", "tensor"),
        P(),
        P("tensor", "dp"),
        P(),
        P(None, "dp", "tensor"),
        P("tensor", "dp"),
    )
    return jax.shard_map(shards, mesh=mesh, in_specs=in_specs, out_specs=out_specs, check_vma=False)
```

```python
import jax
import jax.numpy as jnp
from jax import lax
from jax.sharding import PartitionSpec as P

EPS = 1e-05


def passed_along(block, axis, distance):
    devices = range(lax.axis_size(axis))
    route = [(i - distance, i) for i in devices if i - distance in devices]
    return lax.ppermute(block, axis, route)


def rms_norm(values, gain):
    return values * lax.rsqrt(jnp.mean(values * values, axis=-1, keepdims=True) + EPS) * gain


def rms_back(values, gain, grad_out):
    scale = lax.rsqrt(jnp.mean(values * values, axis=-1, keepdims=True) + EPS)
    normal = values * scale
    weighted = gain * grad_out
    grad_in = scale * (weighted - normal * jnp.mean(normal * weighted, axis=-1, keepdims=True))
    return (grad_in, jnp.sum(normal * grad_out, axis=0))


def times_trans(left, right):
    return lax.dot_general(
        left, right, (((1,), (1,)), ((), ())), preferred_element_type=jnp.float32
    )


def trans_times(left, right):
    return lax.dot_general(
        left, right, (((0,), (0,)), ((), ())), preferred_element_type=jnp.float32
    )


def swapped(block, axis, mask):
    devices = range(lax.axis_size(axis))
    return lax.ppermute(block, axis, [(i, i ^ mask) for i in devices])


def xor_order(blocks, index):
    bit = 1
    while bit < len(blocks):
        flag = (index & bit) > 0
        blocks = [jnp.where(flag, blocks[j ^ bit], blocks[j]) for j in range(len(blocks))]
        bit *= 2
    return blocks


def order_of(count):
    return list(range(0, count, 2)) + list(range(1, count, 2))


def to_relative(values):
    count = lax.axis_size("dp")
    blocks = xor_order(jnp.split(values, count, axis=-1), lax.axis_index("dp"))
    return jnp.concatenate([blocks[j] for j in order_of(count)], axis=-1)


def to_absolute(values):
    count = lax.axis_size("dp")
    places = jnp.split(values, count, axis=-1)
    blocks = [None] * count
    for place, j in enumerate(order_of(count)):
        blocks[j] = places[place]
    return jnp.concatenate(xor_order(blocks, lax.axis_index("dp")), axis=-1)


def gather_weight(shard):
    count = lax.axis_size("dp")
    if count == 8:
        over_x, over_y = yield swapped(shard, "dp", 2), swapped(shard, "dp", 4)
        first, _ = jnp.split(over_x, 2, axis=1)
        _, second = jnp.split(over_y, 2, axis=1)
        first, second = yield swapped(first, "dp", 4), swapped(second, "dp", 2)
        near = jnp.concatenate([shard, over_x, over_y, first, second], axis=1)
    else:
        near = shard
        bit = 2
        while bit < count:
            got = yield swapped(near, "dp", bit)
            near = jnp.concatenate([near, got], axis=1)
            bit *= 2
    far = yield swapped(near, "dp", 1)
    yield None, (near, far)


def beside(values, *pending):
    waited = [(steps, held) for steps, held in pending if not finished(held)]
    values, got = lax.optimization_barrier((values, [held for _, held in waited]))
    got = iter(got)
    moved = [
        (steps, held) if finished(held) else (steps, steps.send(next(got)))
        for steps, held in pending
    ]
    return (values, *moved)


def finished(held):
    return isinstance(held, tuple) and held[0] is None


def begin(steps):
    return steps, next(steps)


def finish(steps, held):
    while not finished(held):
        held = steps.send(held)
    return held[1]


def wide(values):
    return values.astype(jnp.float32)


def narrow(values):
    return values.astype(jnp.bfloat16)


def scatter_weight(near, far):
    count = lax.axis_size("dp")
    got = yield swapped(far, "dp", 1)
    total = wide(near) + wide(got)
    if count == 8:
        own, for_x, for_y, corner = jnp.split(total, 4, axis=1)
        first, second = jnp.split(narrow(corner), 2, axis=1)
        first, second = yield swapped(first, "dp", 2), swapped(second, "dp", 4)
        y_first, y_second = jnp.split(for_y, 2, axis=1)
        x_first, x_second = jnp.split(for_x, 2, axis=1)
        for_y = jnp.concatenate([narrow(y_first + wide(first)), narrow(y_second)], axis=1)
        for_x = jnp.concatenate([narrow(x_first), narrow(x_second + wide(second))], axis=1)
        from_x, from_y = yield swapped(for_x, "dp", 2), swapped(for_y, "dp", 4)
        total = own + wide(from_x) + wide(from_y)
    else:
        bit = count // 2
        while bit > 1:
            keep, send = jnp.split(total, 2, axis=1)
            got = yield swapped(narrow(send), "dp", bit)
            total = keep + wide(got)
            bit //= 2
    yield None, total


def gather_rows(rows):
    return [rows] + [swapped(rows, "tensor", j) for j in range(1, lax.axis_size("tensor"))]


def scatter_rows(blocks):
    total = blocks[0]
    for j in range(1, len(blocks)):
        total = total + wide(swapped(narrow(blocks[j]), "tensor", j))
    return total


def in_token_order(blocks):
    return jnp.concatenate(xor_order(blocks, lax.axis_index("tensor")), axis=0)


def for_owners(rows):
    blocks = jnp.split(rows, lax.axis_size("tensor"), axis=0)
    return xor_order(blocks, lax.axis_index("tensor"))


def summed_over(values, axis):
    count = lax.axis_size(axis)
    if count <= 8:
        blocks = [values] + [swapped(values, axis, j) for j in range(1, count)]
        blocks = xor_order(blocks, lax.axis_index(axis))
        return sum(blocks[1:], blocks[0])
    return lax.psum(values, axis)


def dot(left, right):
    return jnp.dot(left, right, preferred_element_type=jnp.float32)


def halves(values):
    return jnp.split(values, 2, axis=-1)


def shards(
    inputs,
    first_gain,
    entry_projection_weight,
    conv_weight,
    out_weight,
    second_gain,
    gate_up_weight,
    down_weight,
    cotangent,
    lengths,
):
    own_rows = inputs.shape[0]
    group_rows = own_rows * lax.axis_size("tensor")
    channels = entry_projection_weight.shape[2]
    column = lax.axis_index("tensor") * channels
    start = lax.axis_index("dp") * group_rows
    ends = jnp.sum(
        jnp.where(
            jnp.arange(lengths.shape[0])[:, None] >= jnp.arange(lengths.shape[0])[None, :],
            lengths[None, :],
            0,
        ),
        axis=1,
    )
    places = start - 2 + jnp.arange(group_rows + 4, dtype=jnp.int32)
    segment = jnp.sum((places[:, None] >= ends[None, :]).astype(jnp.int32), axis=1)
    first_all = jnp.logical_and(segment[2:] == segment[1:-1], places[2:] >= 1).astype(jnp.float32)[
        :, None
    ]
    second_all = jnp.logical_and(segment[2:] == segment[:-2], places[2:] >= 2).astype(jnp.float32)[
        :, None
    ]
    first_keep = first_all[:group_rows]
    second_keep = second_all[:group_rows]
    kernel = lax.dynamic_slice_in_dim(conv_weight, column, channels, 1)
    mixer_weights = jnp.concatenate([entry_projection_weight, out_weight.T[None]], axis=0)
    mixer_weights, inputs, cotangent = lax.optimization_barrier(
        (mixer_weights, inputs, cotangent)
    )
    mixer_gather = begin(gather_weight(mixer_weights))
    ffn_weights = jnp.concatenate([gate_up_weight, down_weight.T[None]], axis=0)
    ffn_gather = begin(gather_weight(ffn_weights))
    both = to_relative(jnp.concatenate([inputs, cotangent], axis=0))
    residual, cotangent = wide(both[:own_rows]), both[own_rows:]
    first_gain, second_gain = to_relative(jnp.stack([first_gain, second_gain]))
    normed_parts = gather_rows(narrow(rms_norm(residual, first_gain)))
    normed_parts, mixer_gather = beside(normed_parts, mixer_gather)
    grad_parts = gather_rows(cotangent)
    mixer_near, mixer_far = finish(*mixer_gather)
    normed = in_token_order(normed_parts)
    normed, grad_parts = lax.optimization_barrier((normed, grad_parts))

    normed_near, normed_far = halves(normed)
    projected = [
        dot(normed_near, mixer_near[k]) + dot(normed_far, mixer_far[k]) for k in range(3)
    ]
    input_gate_value, c_value, v_value = projected
    product = narrow(input_gate_value * v_value)
    before = passed_along(product[-2:], "dp", 1)
    extended = wide(jnp.concatenate([before, product], axis=0))
    mixed = (
        kernel[2] * extended[2:]
        + kernel[1] * first_keep * extended[1:-1]
        + kernel[0] * second_keep * extended[:-2]
    )
    gated = narrow(c_value * mixed)
    gated, ffn_gather = beside(gated, ffn_gather)
    mixer_part = jnp.concatenate(
        [times_trans(gated, mixer_near[3]), times_trans(gated, mixer_far[3])], axis=1
    )
    middle = residual + scatter_rows(for_owners(mixer_part))
    middle, ffn_gather = beside(middle, ffn_gather)
    grad_rows = jnp.concatenate(grad_parts, axis=0)
    hidden_in = jnp.concatenate(
        gather_rows(narrow(rms_norm(middle, second_gain))), axis=0
    )
    hidden_near, hidden_far = halves(hidden_in)
    ffn_near, ffn_far = finish(*ffn_gather)
    gate_value = dot(hidden_near, ffn_near[0]) + dot(hidden_far, ffn_far[0])
    up_value = dot(hidden_near, ffn_near[1]) + dot(hidden_far, ffn_far[1])
    sigmoid = jax.nn.sigmoid(gate_value)
    swish = gate_value * sigmoid
    hidden = narrow(swish * up_value)
    grad_near, grad_far = halves(grad_rows)
    ffn_part = jnp.concatenate(
        [times_trans(hidden, ffn_near[2]), times_trans(hidden, ffn_far[2])], axis=1
    )
    output = narrow(
        middle + scatter_rows(jnp.split(ffn_part, lax.axis_size("tensor"), axis=0))
    )
    grad_hidden = dot(grad_near, ffn_near[2]) + dot(grad_far, ffn_far[2])
    grad_gate = narrow(grad_hidden * up_value * sigmoid * (1.0 + gate_value * (1.0 - sigmoid)))
    grad_up = narrow(grad_hidden * swish)
    hidden_back = jnp.concatenate(
        [
            times_trans(grad_gate, half[0]) + times_trans(grad_up, half[1])
            for half in (ffn_near, ffn_far)
        ],
        axis=1,
    )
    ffn_scatter = begin(
        scatter_weight(
            *[
                jnp.stack(
                    [
                        narrow(trans_times(rows, grad_gate)),
                        narrow(trans_times(rows, grad_up)),
                        narrow(trans_times(outer, hidden)),
                    ]
                )
                for rows, outer in ((hidden_near, grad_near), (hidden_far, grad_far))
            ]
        )
    )
    hidden_back, output = lax.optimization_barrier((hidden_back, output))
    grad_hin = scatter_rows(jnp.split(hidden_back, lax.axis_size("tensor"), axis=0))
    grad_hin, ffn_scatter = beside(grad_hin, ffn_scatter)
    second_back, second_part = rms_back(middle, second_gain, grad_hin)
    grad_middle = wide(cotangent) + second_back
    branch_rows = in_token_order(gather_rows(narrow(grad_middle)))
    branch_rows, ffn_scatter = beside(branch_rows, ffn_scatter)
    branch_near, branch_far = halves(branch_rows)
    grad_gated = dot(branch_near, mixer_near[3]) + dot(branch_far, mixer_far[3])
    output_gate_gradient = narrow(grad_gated * mixed)
    grad_mixed = narrow(grad_gated * c_value)
    after = passed_along(grad_mixed[:2], "dp", -1)
    grad_ext = wide(jnp.concatenate([grad_mixed, after], axis=0))
    mixed_wide = grad_ext[:-2]
    kernel_part = jnp.stack(
        [
            jnp.sum(second_keep * extended[:-2] * mixed_wide, axis=0),
            jnp.sum(first_keep * extended[1:-1] * mixed_wide, axis=0),
            jnp.sum(extended[2:] * mixed_wide, axis=0),
        ]
    )
    kernel_full = lax.dynamic_update_slice_in_dim(
        jnp.zeros(conv_weight.shape, jnp.float32), kernel_part, column, 1
    )
    elementwise_product_gradient = (
        kernel[2] * grad_ext[:-2]
        + kernel[1] * first_all[1:-1] * grad_ext[1:-1]
        + kernel[0] * second_all[2:] * grad_ext[2:]
    )
    input_gate_gradient = narrow(elementwise_product_gradient * v_value)
    value_branch_gradient = narrow(elementwise_product_gradient * input_gate_value)
    grads = [input_gate_gradient, output_gate_gradient, value_branch_gradient]
    mixer_scatter = begin(
        scatter_weight(
            *[
                jnp.stack(
                    [narrow(trans_times(rows, grad)) for grad in grads]
                    + [narrow(trans_times(outer, gated))]
                )
                for rows, outer in ((normed_near, branch_near), (normed_far, branch_far))
            ]
        )
    )
    normed_back = jnp.concatenate(
        [
            sum(times_trans(grads[k], half[k]) for k in range(3))
            for half in (mixer_near, mixer_far)
        ],
        axis=1,
    )
    grad_normed = scatter_rows(for_owners(normed_back))
    grad_normed, ffn_scatter, mixer_scatter = beside(grad_normed, ffn_scatter, mixer_scatter)
    first_back, first_part = rms_back(residual, first_gain, grad_normed)
    input_grad = grad_middle + first_back
    small = jnp.concatenate(
        [to_absolute(first_part)[None], to_absolute(second_part)[None], kernel_full], axis=0
    )
    small = summed_over(small, "tensor")
    small, mixer_scatter = beside(small, mixer_scatter)
    small = summed_over(small, "dp")
    ffn_grad = finish(*ffn_scatter)
    mixer_grad = finish(*mixer_scatter)
    return (
        to_absolute(output),
        to_absolute(input_grad),
        small[0],
        mixer_grad[:3],
        small[2:],
        mixer_grad[3].T,
        small[1],
        ffn_grad[:2],
        ffn_grad[2].T,
    )


def solution(mesh):
    in_specs = (
        P(("dp", "tensor"), None),
        P(),
        P(None, "dp", "tensor"),
        P(),
        P("tensor", "dp"),
        P(),
        P(None, "dp", "tensor"),
        P("tensor", "dp"),
        P(("dp", "tensor"), None),
        P(),
    )
    out_specs = (
        P(("dp", "tensor"), None),
        P(("dp", "tensor"), None),
        P(),
        P(None, "dp", "tensor"),
        P(),
        P("tensor", "dp"),
        P(),
        P(None, "dp", "tensor"),
        P("tensor", "dp"),
    )
    return jax.shard_map(shards, mesh=mesh, in_specs=in_specs, out_specs=out_specs, check_vma=False)
```

```python
import jax
import jax.numpy as jnp
from jax import lax
from jax.sharding import PartitionSpec as P

EPS = 1e-05


def passed_along(block, axis, distance):
    devices = range(lax.axis_size(axis))
    route = [(i - distance, i) for i in devices if i - distance in devices]
    return lax.ppermute(block, axis, route)


def rms_norm(values, gain):
    return values * lax.rsqrt(jnp.mean(values * values, axis=-1, keepdims=True) + EPS) * gain


def rms_back(values, gain, grad_out):
    scale = lax.rsqrt(jnp.mean(values * values, axis=-1, keepdims=True) + EPS)
    normal = values * scale
    weighted = gain * grad_out
    grad_in = scale * (weighted - normal * jnp.mean(normal * weighted, axis=-1, keepdims=True))
    return (grad_in, jnp.sum(normal * grad_out, axis=0))


def times_trans(left, right):
    return lax.dot_general(
        left, right, (((1,), (1,)), ((), ())), preferred_element_type=jnp.float32
    )


def trans_times(left, right):
    return lax.dot_general(
        left, right, (((0,), (0,)), ((), ())), preferred_element_type=jnp.float32
    )


def swapped(block, axis, mask):
    devices = range(lax.axis_size(axis))
    return lax.ppermute(block, axis, [(i, i ^ mask) for i in devices])


def xor_order(blocks, index):
    bit = 1
    while bit < len(blocks):
        flag = (index & bit) > 0
        blocks = [jnp.where(flag, blocks[j ^ bit], blocks[j]) for j in range(len(blocks))]
        bit *= 2
    return blocks


def order_of(count):
    return list(range(0, count, 2)) + list(range(1, count, 2))


def to_relative(values):
    count = lax.axis_size("dp")
    blocks = xor_order(jnp.split(values, count, axis=-1), lax.axis_index("dp"))
    return jnp.concatenate([blocks[j] for j in order_of(count)], axis=-1)


def to_absolute(values):
    count = lax.axis_size("dp")
    places = jnp.split(values, count, axis=-1)
    blocks = [None] * count
    for place, j in enumerate(order_of(count)):
        blocks[j] = places[place]
    return jnp.concatenate(xor_order(blocks, lax.axis_index("dp")), axis=-1)


def gather_weight(shard):
    count = lax.axis_size("dp")
    if count == 8:
        over_x, over_y = yield swapped(shard, "dp", 2), swapped(shard, "dp", 4)
        first, _ = jnp.split(over_x, 2, axis=1)
        _, second = jnp.split(over_y, 2, axis=1)
        first, second = yield swapped(first, "dp", 4), swapped(second, "dp", 2)
        near = jnp.concatenate([shard, over_x, over_y, first, second], axis=1)
    else:
        near = shard
        bit = 2
        while bit < count:
            got = yield swapped(near, "dp", bit)
            near = jnp.concatenate([near, got], axis=1)
            bit *= 2
    far = yield swapped(near, "dp", 1)
    yield None, (near, far)


def beside(values, *pending):
    waited = [(steps, held) for steps, held in pending if not finished(held)]
    values, got = lax.optimization_barrier((values, [held for _, held in waited]))
    got = iter(got)
    moved = [
        (steps, held) if finished(held) else (steps, steps.send(next(got)))
        for steps, held in pending
    ]
    return (values, *moved)


def finished(held):
    return isinstance(held, tuple) and held[0] is None


def begin(steps):
    return steps, next(steps)


def finish(steps, held):
    while not finished(held):
        held = steps.send(held)
    return held[1]


def wide(values):
    return values.astype(jnp.float32)


def narrow(values):
    return values.astype(jnp.bfloat16)


def scatter_weight(near, far):
    count = lax.axis_size("dp")
    got = yield swapped(far, "dp", 1)
    total = wide(near) + wide(got)
    if count == 8:
        own, for_x, for_y, corner = jnp.split(total, 4, axis=1)
        first, second = jnp.split(narrow(corner), 2, axis=1)
        first, second = yield swapped(first, "dp", 2), swapped(second, "dp", 4)
        y_first, y_second = jnp.split(for_y, 2, axis=1)
        x_first, x_second = jnp.split(for_x, 2, axis=1)
        for_y = jnp.concatenate([narrow(y_first + wide(first)), narrow(y_second)], axis=1)
        for_x = jnp.concatenate([narrow(x_first), narrow(x_second + wide(second))], axis=1)
        from_x, from_y = yield swapped(for_x, "dp", 2), swapped(for_y, "dp", 4)
        total = own + wide(from_x) + wide(from_y)
    else:
        bit = count // 2
        while bit > 1:
            keep, send = jnp.split(total, 2, axis=1)
            got = yield swapped(narrow(send), "dp", bit)
            total = keep + wide(got)
            bit //= 2
    yield None, total


def gather_rows(rows):
    return [rows] + [swapped(rows, "tensor", j) for j in range(1, lax.axis_size("tensor"))]


def scatter_rows(blocks):
    total = blocks[0]
    for j in range(1, len(blocks)):
        total = total + wide(swapped(narrow(blocks[j]), "tensor", j))
    return total


def in_token_order(blocks):
    return jnp.concatenate(xor_order(blocks, lax.axis_index("tensor")), axis=0)


def for_owners(rows):
    blocks = jnp.split(rows, lax.axis_size("tensor"), axis=0)
    return xor_order(blocks, lax.axis_index("tensor"))


def summed_over(values, axis):
    count = lax.axis_size(axis)
    if count <= 8:
        blocks = [values] + [swapped(values, axis, j) for j in range(1, count)]
        blocks = xor_order(blocks, lax.axis_index(axis))
        return sum(blocks[1:], blocks[0])
    return lax.psum(values, axis)


def dot(left, right):
    return jnp.dot(left, right, preferred_element_type=jnp.float32)


def halves(values):
    return jnp.split(values, 2, axis=-1)


def shards(
    inputs,
    first_gain,
    entry_projection_weight,
    conv_weight,
    out_weight,
    second_gain,
    gate_up_weight,
    down_weight,
    cotangent,
    lengths,
):
    own_rows = inputs.shape[0]
    group_rows = own_rows * lax.axis_size("tensor")
    channels = entry_projection_weight.shape[2]
    column = lax.axis_index("tensor") * channels
    start = lax.axis_index("dp") * group_rows
    ends = jnp.sum(
        jnp.where(
            jnp.arange(lengths.shape[0])[:, None] >= jnp.arange(lengths.shape[0])[None, :],
            lengths[None, :],
            0,
        ),
        axis=1,
    )
    places = start - 2 + jnp.arange(group_rows + 4, dtype=jnp.int32)
    segment = jnp.sum((places[:, None] >= ends[None, :]).astype(jnp.int32), axis=1)
    first_all = jnp.logical_and(segment[2:] == segment[1:-1], places[2:] >= 1).astype(jnp.float32)[
        :, None
    ]
    second_all = jnp.logical_and(segment[2:] == segment[:-2], places[2:] >= 2).astype(jnp.float32)[
        :, None
    ]
    first_keep = first_all[:group_rows]
    second_keep = second_all[:group_rows]
    kernel = lax.dynamic_slice_in_dim(conv_weight, column, channels, 1)
    mixer_weights = jnp.concatenate([entry_projection_weight, out_weight.T[None]], axis=0)
    mixer_weights, inputs, cotangent = lax.optimization_barrier(
        (mixer_weights, inputs, cotangent)
    )
    mixer_gather = begin(gather_weight(mixer_weights))
    ffn_weights = jnp.concatenate([gate_up_weight, down_weight.T[None]], axis=0)
    ffn_gather = begin(gather_weight(ffn_weights))
    both = to_relative(jnp.concatenate([inputs, cotangent], axis=0))
    residual, cotangent = wide(both[:own_rows]), both[own_rows:]
    first_gain, second_gain = to_relative(jnp.stack([first_gain, second_gain]))
    normed_parts = gather_rows(narrow(rms_norm(residual, first_gain)))
    normed_parts, mixer_gather = beside(normed_parts, mixer_gather)
    grad_parts = gather_rows(cotangent)
    mixer_near, mixer_far = finish(*mixer_gather)
    normed = in_token_order(normed_parts)
    (normed, grad_parts), ffn_gather = beside((normed, grad_parts), ffn_gather)

    normed_near, normed_far = halves(normed)
    projected = [
        dot(normed_near, mixer_near[k]) + dot(normed_far, mixer_far[k]) for k in range(3)
    ]
    input_gate_value, c_value, v_value = projected
    product = narrow(input_gate_value * v_value)
    before = passed_along(product[-2:], "dp", 1)
    extended = wide(jnp.concatenate([before, product], axis=0))
    mixed = (
        kernel[2] * extended[2:]
        + kernel[1] * first_keep * extended[1:-1]
        + kernel[0] * second_keep * extended[:-2]
    )
    gated = narrow(c_value * mixed)
    gated, ffn_gather = beside(gated, ffn_gather)
    mixer_part = jnp.concatenate(
        [times_trans(gated, mixer_near[3]), times_trans(gated, mixer_far[3])], axis=1
    )
    middle = residual + scatter_rows(for_owners(mixer_part))
    grad_rows = jnp.concatenate(grad_parts, axis=0)
    hidden_in = jnp.concatenate(
        gather_rows(narrow(rms_norm(middle, second_gain))), axis=0
    )
    hidden_near, hidden_far = halves(hidden_in)
    ffn_near, ffn_far = finish(*ffn_gather)
    gate_value = dot(hidden_near, ffn_near[0]) + dot(hidden_far, ffn_far[0])
    up_value = dot(hidden_near, ffn_near[1]) + dot(hidden_far, ffn_far[1])
    sigmoid = jax.nn.sigmoid(gate_value)
    swish = gate_value * sigmoid
    hidden = narrow(swish * up_value)
    grad_near, grad_far = halves(grad_rows)
    ffn_part = jnp.concatenate(
        [times_trans(hidden, ffn_near[2]), times_trans(hidden, ffn_far[2])], axis=1
    )
    output = narrow(
        middle + scatter_rows(jnp.split(ffn_part, lax.axis_size("tensor"), axis=0))
    )
    grad_hidden = dot(grad_near, ffn_near[2]) + dot(grad_far, ffn_far[2])
    grad_gate = narrow(grad_hidden * up_value * sigmoid * (1.0 + gate_value * (1.0 - sigmoid)))
    grad_up = narrow(grad_hidden * swish)
    hidden_back = jnp.concatenate(
        [
            times_trans(grad_gate, half[0]) + times_trans(grad_up, half[1])
            for half in (ffn_near, ffn_far)
        ],
        axis=1,
    )
    ffn_scatter = begin(
        scatter_weight(
            *[
                jnp.stack(
                    [
                        narrow(trans_times(rows, grad_gate)),
                        narrow(trans_times(rows, grad_up)),
                        narrow(trans_times(outer, hidden)),
                    ]
                )
                for rows, outer in ((hidden_near, grad_near), (hidden_far, grad_far))
            ]
        )
    )
    hidden_back, output = lax.optimization_barrier((hidden_back, output))
    grad_hin = scatter_rows(jnp.split(hidden_back, lax.axis_size("tensor"), axis=0))
    grad_hin, ffn_scatter = beside(grad_hin, ffn_scatter)
    second_back, second_part = rms_back(middle, second_gain, grad_hin)
    grad_middle = wide(cotangent) + second_back
    branch_rows = in_token_order(gather_rows(narrow(grad_middle)))
    branch_rows, ffn_scatter = beside(branch_rows, ffn_scatter)
    branch_near, branch_far = halves(branch_rows)
    grad_gated = dot(branch_near, mixer_near[3]) + dot(branch_far, mixer_far[3])
    output_gate_gradient = narrow(grad_gated * mixed)
    grad_mixed = narrow(grad_gated * c_value)
    after = passed_along(grad_mixed[:2], "dp", -1)
    grad_ext = wide(jnp.concatenate([grad_mixed, after], axis=0))
    mixed_wide = grad_ext[:-2]
    kernel_part = jnp.stack(
        [
            jnp.sum(second_keep * extended[:-2] * mixed_wide, axis=0),
            jnp.sum(first_keep * extended[1:-1] * mixed_wide, axis=0),
            jnp.sum(extended[2:] * mixed_wide, axis=0),
        ]
    )
    kernel_full = lax.dynamic_update_slice_in_dim(
        jnp.zeros(conv_weight.shape, jnp.float32), kernel_part, column, 1
    )
    elementwise_product_gradient = (
        kernel[2] * grad_ext[:-2]
        + kernel[1] * first_all[1:-1] * grad_ext[1:-1]
        + kernel[0] * second_all[2:] * grad_ext[2:]
    )
    input_gate_gradient = narrow(elementwise_product_gradient * v_value)
    value_branch_gradient = narrow(elementwise_product_gradient * input_gate_value)
    grads = [input_gate_gradient, output_gate_gradient, value_branch_gradient]
    mixer_scatter = begin(
        scatter_weight(
            *[
                jnp.stack(
                    [narrow(trans_times(rows, grad)) for grad in grads]
                    + [narrow(trans_times(outer, gated))]
                )
                for rows, outer in ((normed_near, branch_near), (normed_far, branch_far))
            ]
        )
    )
    normed_back = jnp.concatenate(
        [
            sum(times_trans(grads[k], half[k]) for k in range(3))
            for half in (mixer_near, mixer_far)
        ],
        axis=1,
    )
    normed_back, mixer_scatter = beside(normed_back, mixer_scatter)
    grad_normed = scatter_rows(for_owners(normed_back))
    grad_normed, ffn_scatter, mixer_scatter = beside(grad_normed, ffn_scatter, mixer_scatter)
    first_back, first_part = rms_back(residual, first_gain, grad_normed)
    input_grad = grad_middle + first_back
    small = jnp.concatenate(
        [to_absolute(first_part)[None], to_absolute(second_part)[None], kernel_full], axis=0
    )
    small = summed_over(small, "tensor")
    small, mixer_scatter = beside(small, mixer_scatter)
    small = summed_over(small, "dp")
    ffn_grad = finish(*ffn_scatter)
    mixer_grad = finish(*mixer_scatter)
    return (
        to_absolute(output),
        to_absolute(input_grad),
        small[0],
        mixer_grad[:3],
        small[2:],
        mixer_grad[3].T,
        small[1],
        ffn_grad[:2],
        ffn_grad[2].T,
    )


def solution(mesh):
    in_specs = (
        P(("dp", "tensor"), None),
        P(),
        P(None, "dp", "tensor"),
        P(),
        P("tensor", "dp"),
        P(),
        P(None, "dp", "tensor"),
        P("tensor", "dp"),
        P(("dp", "tensor"), None),
        P(),
    )
    out_specs = (
        P(("dp", "tensor"), None),
        P(("dp", "tensor"), None),
        P(),
        P(None, "dp", "tensor"),
        P(),
        P("tensor", "dp"),
        P(),
        P(None, "dp", "tensor"),
        P("tensor", "dp"),
    )
    return jax.shard_map(shards, mesh=mesh, in_specs=in_specs, out_specs=out_specs, check_vma=False)
```

```python
import jax
import jax.numpy as jnp
from jax import lax
from jax.sharding import PartitionSpec as P

EPS = 1e-05


def passed_along(block, axis, distance):
    devices = range(lax.axis_size(axis))
    route = [(i - distance, i) for i in devices if i - distance in devices]
    return lax.ppermute(block, axis, route)


def rms_norm(values, gain):
    return values * lax.rsqrt(jnp.mean(values * values, axis=-1, keepdims=True) + EPS) * gain


def rms_back(values, gain, grad_out):
    scale = lax.rsqrt(jnp.mean(values * values, axis=-1, keepdims=True) + EPS)
    normal = values * scale
    weighted = gain * grad_out
    grad_in = scale * (weighted - normal * jnp.mean(normal * weighted, axis=-1, keepdims=True))
    return (grad_in, jnp.sum(normal * grad_out, axis=0))


def times_trans(left, right):
    return lax.dot_general(
        left, right, (((1,), (1,)), ((), ())), preferred_element_type=jnp.float32
    )


def trans_times(left, right):
    return lax.dot_general(
        left, right, (((0,), (0,)), ((), ())), preferred_element_type=jnp.float32
    )


def swapped(block, axis, mask):
    devices = range(lax.axis_size(axis))
    return lax.ppermute(block, axis, [(i, i ^ mask) for i in devices])


def xor_order(blocks, index):
    bit = 1
    while bit < len(blocks):
        flag = (index & bit) > 0
        blocks = [jnp.where(flag, blocks[j ^ bit], blocks[j]) for j in range(len(blocks))]
        bit *= 2
    return blocks


def order_of(count):
    return list(range(0, count, 2)) + list(range(1, count, 2))


def to_relative(values):
    count = lax.axis_size("dp")
    blocks = xor_order(jnp.split(values, count, axis=-1), lax.axis_index("dp"))
    return jnp.concatenate([blocks[j] for j in order_of(count)], axis=-1)


def to_absolute(values):
    count = lax.axis_size("dp")
    places = jnp.split(values, count, axis=-1)
    blocks = [None] * count
    for place, j in enumerate(order_of(count)):
        blocks[j] = places[place]
    return jnp.concatenate(xor_order(blocks, lax.axis_index("dp")), axis=-1)


def gather_weight(shard):
    count = lax.axis_size("dp")
    if count == 8:
        over_x, over_y = yield swapped(shard, "dp", 2), swapped(shard, "dp", 4)
        first, _ = jnp.split(over_x, 2, axis=1)
        _, second = jnp.split(over_y, 2, axis=1)
        first, second = yield swapped(first, "dp", 4), swapped(second, "dp", 2)
        near = jnp.concatenate([shard, over_x, over_y, first, second], axis=1)
    else:
        near = shard
        bit = 2
        while bit < count:
            got = yield swapped(near, "dp", bit)
            near = jnp.concatenate([near, got], axis=1)
            bit *= 2
    far = yield swapped(near, "dp", 1)
    yield None, (near, far)


def beside(values, *pending):
    waited = [(steps, held) for steps, held in pending if not finished(held)]
    values, got = lax.optimization_barrier((values, [held for _, held in waited]))
    got = iter(got)
    moved = [
        (steps, held) if finished(held) else (steps, steps.send(next(got)))
        for steps, held in pending
    ]
    return (values, *moved)


def finished(held):
    return isinstance(held, tuple) and held[0] is None


def begin(steps):
    return steps, next(steps)


def finish(steps, held):
    while not finished(held):
        held = steps.send(held)
    return held[1]


def wide(values):
    return values.astype(jnp.float32)


def narrow(values):
    return values.astype(jnp.bfloat16)


def scatter_weight(near, far):
    count = lax.axis_size("dp")
    got = yield swapped(far, "dp", 1)
    total = wide(near) + wide(got)
    if count == 8:
        own, for_x, for_y, corner = jnp.split(total, 4, axis=1)
        first, second = jnp.split(narrow(corner), 2, axis=1)
        first, second = yield swapped(first, "dp", 2), swapped(second, "dp", 4)
        y_first, y_second = jnp.split(for_y, 2, axis=1)
        x_first, x_second = jnp.split(for_x, 2, axis=1)
        for_y = jnp.concatenate([narrow(y_first + wide(first)), narrow(y_second)], axis=1)
        for_x = jnp.concatenate([narrow(x_first), narrow(x_second + wide(second))], axis=1)
        from_x, from_y = yield swapped(for_x, "dp", 2), swapped(for_y, "dp", 4)
        total = own + wide(from_x) + wide(from_y)
    else:
        bit = count // 2
        while bit > 1:
            keep, send = jnp.split(total, 2, axis=1)
            got = yield swapped(narrow(send), "dp", bit)
            total = keep + wide(got)
            bit //= 2
    yield None, total


def gather_rows(rows):
    return [rows] + [swapped(rows, "tensor", j) for j in range(1, lax.axis_size("tensor"))]


def scatter_rows(blocks):
    total = blocks[0]
    for j in range(1, len(blocks)):
        total = total + wide(swapped(narrow(blocks[j]), "tensor", j))
    return total


def in_token_order(blocks):
    return jnp.concatenate(xor_order(blocks, lax.axis_index("tensor")), axis=0)


def for_owners(rows):
    blocks = jnp.split(rows, lax.axis_size("tensor"), axis=0)
    return xor_order(blocks, lax.axis_index("tensor"))


def summed_over(values, axis):
    count = lax.axis_size(axis)
    if count <= 8:
        blocks = [values] + [swapped(values, axis, j) for j in range(1, count)]
        blocks = xor_order(blocks, lax.axis_index(axis))
        return sum(blocks[1:], blocks[0])
    return lax.psum(values, axis)


def dot(left, right):
    return jnp.dot(left, right, preferred_element_type=jnp.float32)


def halves(values):
    return jnp.split(values, 2, axis=-1)


def shards(
    inputs,
    first_gain,
    entry_projection_weight,
    conv_weight,
    out_weight,
    second_gain,
    gate_up_weight,
    down_weight,
    cotangent,
    lengths,
):
    own_rows = inputs.shape[0]
    group_rows = own_rows * lax.axis_size("tensor")
    channels = entry_projection_weight.shape[2]
    column = lax.axis_index("tensor") * channels
    start = lax.axis_index("dp") * group_rows
    ends = jnp.sum(
        jnp.where(
            jnp.arange(lengths.shape[0])[:, None] >= jnp.arange(lengths.shape[0])[None, :],
            lengths[None, :],
            0,
        ),
        axis=1,
    )
    places = start - 2 + jnp.arange(group_rows + 4, dtype=jnp.int32)
    segment = jnp.sum((places[:, None] >= ends[None, :]).astype(jnp.int32), axis=1)
    first_all = jnp.logical_and(segment[2:] == segment[1:-1], places[2:] >= 1).astype(jnp.float32)[
        :, None
    ]
    second_all = jnp.logical_and(segment[2:] == segment[:-2], places[2:] >= 2).astype(jnp.float32)[
        :, None
    ]
    first_keep = first_all[:group_rows]
    second_keep = second_all[:group_rows]
    kernel = lax.dynamic_slice_in_dim(conv_weight, column, channels, 1)
    mixer_weights = jnp.concatenate([entry_projection_weight, out_weight.T[None]], axis=0)
    mixer_weights, inputs, cotangent = lax.optimization_barrier(
        (mixer_weights, inputs, cotangent)
    )
    mixer_gather = begin(gather_weight(mixer_weights))
    ffn_weights = jnp.concatenate([gate_up_weight, down_weight.T[None]], axis=0)
    ffn_gather = begin(gather_weight(ffn_weights))
    both = to_relative(jnp.concatenate([inputs, cotangent], axis=0))
    residual, cotangent = wide(both[:own_rows]), both[own_rows:]
    first_gain, second_gain = to_relative(jnp.stack([first_gain, second_gain]))
    normed_parts = gather_rows(narrow(rms_norm(residual, first_gain)))
    normed_parts, mixer_gather = beside(normed_parts, mixer_gather)
    grad_parts = gather_rows(cotangent)
    mixer_near, mixer_far = finish(*mixer_gather)
    normed = in_token_order(normed_parts)
    (normed, grad_parts), ffn_gather = beside((normed, grad_parts), ffn_gather)

    normed_near, normed_far = halves(normed)
    projected = [
        dot(normed_near, mixer_near[k]) + dot(normed_far, mixer_far[k]) for k in range(3)
    ]
    input_gate_value, c_value, v_value = projected
    product = narrow(input_gate_value * v_value)
    before = passed_along(product[-2:], "dp", 1)
    extended = wide(jnp.concatenate([before, product], axis=0))
    mixed = (
        kernel[2] * extended[2:]
        + kernel[1] * first_keep * extended[1:-1]
        + kernel[0] * second_keep * extended[:-2]
    )
    gated = narrow(c_value * mixed)
    mixer_part = jnp.concatenate(
        [times_trans(gated, mixer_near[3]), times_trans(gated, mixer_far[3])], axis=1
    )
    middle = residual + scatter_rows(for_owners(mixer_part))
    middle, ffn_gather = beside(middle, ffn_gather)
    grad_rows = jnp.concatenate(grad_parts, axis=0)
    hidden_in = jnp.concatenate(
        gather_rows(narrow(rms_norm(middle, second_gain))), axis=0
    )
    hidden_near, hidden_far = halves(hidden_in)
    ffn_near, ffn_far = finish(*ffn_gather)
    gate_value = dot(hidden_near, ffn_near[0]) + dot(hidden_far, ffn_far[0])
    up_value = dot(hidden_near, ffn_near[1]) + dot(hidden_far, ffn_far[1])
    sigmoid = jax.nn.sigmoid(gate_value)
    swish = gate_value * sigmoid
    hidden = narrow(swish * up_value)
    grad_near, grad_far = halves(grad_rows)
    ffn_part = jnp.concatenate(
        [times_trans(hidden, ffn_near[2]), times_trans(hidden, ffn_far[2])], axis=1
    )
    output = narrow(
        middle + scatter_rows(jnp.split(ffn_part, lax.axis_size("tensor"), axis=0))
    )
    grad_hidden = dot(grad_near, ffn_near[2]) + dot(grad_far, ffn_far[2])
    grad_gate = narrow(grad_hidden * up_value * sigmoid * (1.0 + gate_value * (1.0 - sigmoid)))
    grad_up = narrow(grad_hidden * swish)
    hidden_back = jnp.concatenate(
        [
            times_trans(grad_gate, half[0]) + times_trans(grad_up, half[1])
            for half in (ffn_near, ffn_far)
        ],
        axis=1,
    )
    ffn_scatter = begin(
        scatter_weight(
            *[
                jnp.stack(
                    [
                        narrow(trans_times(rows, grad_gate)),
                        narrow(trans_times(rows, grad_up)),
                        narrow(trans_times(outer, hidden)),
                    ]
                )
                for rows, outer in ((hidden_near, grad_near), (hidden_far, grad_far))
            ]
        )
    )
    hidden_back, output = lax.optimization_barrier((hidden_back, output))
    grad_hin = scatter_rows(jnp.split(hidden_back, lax.axis_size("tensor"), axis=0))
    grad_hin, ffn_scatter = beside(grad_hin, ffn_scatter)
    second_back, second_part = rms_back(middle, second_gain, grad_hin)
    grad_middle = wide(cotangent) + second_back
    branch_rows = in_token_order(gather_rows(narrow(grad_middle)))
    branch_rows, ffn_scatter = beside(branch_rows, ffn_scatter)
    branch_near, branch_far = halves(branch_rows)
    grad_gated = dot(branch_near, mixer_near[3]) + dot(branch_far, mixer_far[3])
    output_gate_gradient = narrow(grad_gated * mixed)
    grad_mixed = narrow(grad_gated * c_value)
    after = passed_along(grad_mixed[:2], "dp", -1)
    grad_ext = wide(jnp.concatenate([grad_mixed, after], axis=0))
    mixed_wide = grad_ext[:-2]
    kernel_part = jnp.stack(
        [
            jnp.sum(second_keep * extended[:-2] * mixed_wide, axis=0),
            jnp.sum(first_keep * extended[1:-1] * mixed_wide, axis=0),
            jnp.sum(extended[2:] * mixed_wide, axis=0),
        ]
    )
    kernel_full = lax.dynamic_update_slice_in_dim(
        jnp.zeros(conv_weight.shape, jnp.float32), kernel_part, column, 1
    )
    elementwise_product_gradient = (
        kernel[2] * grad_ext[:-2]
        + kernel[1] * first_all[1:-1] * grad_ext[1:-1]
        + kernel[0] * second_all[2:] * grad_ext[2:]
    )
    input_gate_gradient = narrow(elementwise_product_gradient * v_value)
    value_branch_gradient = narrow(elementwise_product_gradient * input_gate_value)
    grads = [input_gate_gradient, output_gate_gradient, value_branch_gradient]
    mixer_scatter = begin(
        scatter_weight(
            *[
                jnp.stack(
                    [narrow(trans_times(rows, grad)) for grad in grads]
                    + [narrow(trans_times(outer, gated))]
                )
                for rows, outer in ((normed_near, branch_near), (normed_far, branch_far))
            ]
        )
    )
    normed_back = jnp.concatenate(
        [
            sum(times_trans(grads[k], half[k]) for k in range(3))
            for half in (mixer_near, mixer_far)
        ],
        axis=1,
    )
    normed_back, mixer_scatter = beside(normed_back, mixer_scatter)
    grad_normed = scatter_rows(for_owners(normed_back))
    grad_normed, ffn_scatter, mixer_scatter = beside(grad_normed, ffn_scatter, mixer_scatter)
    first_back, first_part = rms_back(residual, first_gain, grad_normed)
    input_grad = grad_middle + first_back
    small = jnp.concatenate(
        [to_absolute(first_part)[None], to_absolute(second_part)[None], kernel_full], axis=0
    )
    small = summed_over(small, "tensor")
    small, mixer_scatter = beside(small, mixer_scatter)
    small = summed_over(small, "dp")
    ffn_grad = finish(*ffn_scatter)
    mixer_grad = finish(*mixer_scatter)
    return (
        to_absolute(output),
        to_absolute(input_grad),
        small[0],
        mixer_grad[:3],
        small[2:],
        mixer_grad[3].T,
        small[1],
        ffn_grad[:2],
        ffn_grad[2].T,
    )


def solution(mesh):
    in_specs = (
        P(("dp", "tensor"), None),
        P(),
        P(None, "dp", "tensor"),
        P(),
        P("tensor", "dp"),
        P(),
        P(None, "dp", "tensor"),
        P("tensor", "dp"),
        P(("dp", "tensor"), None),
        P(),
    )
    out_specs = (
        P(("dp", "tensor"), None),
        P(("dp", "tensor"), None),
        P(),
        P(None, "dp", "tensor"),
        P(),
        P("tensor", "dp"),
        P(),
        P(None, "dp", "tensor"),
        P("tensor", "dp"),
    )
    return jax.shard_map(shards, mesh=mesh, in_specs=in_specs, out_specs=out_specs, check_vma=False)
```
